32 devices in a mesh: dp: 8 (over y, x, core), tensor: 4 (over z).
Axes of the slice: x: 2, y: 2, z: 4, core: 2. Of those that a mesh axis runs over, the one named last changes fastest.
Arguments:
- act_codes: int32 [4096, 28672], P('dp', 'tensor'), may hold values from 40 to 199, as said below
- grad_codes: int32 [4096, 4096], P(('dp', 'tensor')), may hold values from 40 to 199, as said below
- amax_history: float32 [32, 1024], P(('dp', 'tensor')), may hold values from 0.001953125 to 96, as said below
Outputs:
- weight_grad: float32 [28672, 4096], P('tensor', 'dp')
- new_history: float32 [32, 1024], P(('dp', 'tensor'))
The draws below stay inside these ranges and needn't reach their ends.
Inputs may be any that keep to these rules, and one draw needn't show every extreme that they name: `act_codes`: each code is 128 s + 8 e + m with a sign bit s of 0 or 1, an exponent field e of 5 to 8 and a mantissa m of 0 to 7. `grad_codes`: each code is 128 s + 8 e + m with a sign bit s of 0 or 1, an exponent field e of 5 to 8 and a mantissa m of 0 to 7. `amax_history`: every entry is a whole number times a power of two; the largest entry of the array is (192) times 1/8, 1/4 or 1/2.
All inputs are finite; a program needn't handle non-finite values.
Results may differ from the reference program's by a relative error of at most 0.0003.
Values may be sent and summed in bfloat16 or wider, within the bound.
A program may use at most 192 MiB of HBM per device.

```python
import jax
import jax.numpy as jnp
from jax import lax

FF = 28672
PANEL = 4096
TOK_DEV = 512
HIST = 1024
TOKENS = 4096
RANKS = 32
LEVELS = 3
N_DP = 8
N_TENSOR = 4


def make_codes(key, shape):
    sign_key, exponent_key, mantissa_key = jax.random.split(key, 3)
    sign_bit = jax.random.randint(sign_key, shape, 0, 2)
    exponent_field = jax.random.randint(exponent_key, shape, 5, 9)
    mantissa = jax.random.randint(mantissa_key, shape, 0, 8)
    return (sign_bit * 128 + exponent_field * 8 + mantissa).astype(jnp.int32)


def draw_act_codes(key, part):
    key = jax.random.fold_in(key, 1)
    return make_codes(key, (TOKENS, FF))


def draw_grad_codes(key, part):
    key = jax.random.fold_in(key, 2)
    return make_codes(key, (TOKENS, PANEL))


def draw_amax_history(key, part):
    key = jax.random.fold_in(key, 3)
    subkeys = jax.random.split(key, 5)
    integers = jax.random.randint(subkeys[0], (RANKS, HIST), 1, 128).astype(jnp.float32)
    shift_index = jax.random.randint(subkeys[1], (RANKS, HIST), 0, 4)
    powers = jnp.array([2.0 ** (-9), 2.0 ** (-8), 2.0 ** (-7), 2.0 ** (-6)], jnp.float32)
    drawn = integers * powers[shift_index]
    top_index = jax.random.randint(subkeys[2], (), 0, 3)
    top_value = (TOK_DEV // 4 + 64) * jnp.array([0.125, 0.25, 0.5], jnp.float32)[top_index]
    row_pick = jax.random.randint(subkeys[3], (), 0, RANKS)
    column_pick = jax.random.randint(subkeys[4], (), 0, HIST)
    row_index = jnp.arange(RANKS)[:, None]
    column_index = jnp.arange(HIST)[None, :]
    chosen = (row_index == row_pick) & (column_index == column_pick)
    return jnp.where(chosen, top_value, drawn).astype(jnp.float32)


def setup_inputs(seed: int = 0) -> dict:
    keys = jax.random.split(jax.random.key(seed), 4)
    act_codes = draw_act_codes(jax.random.fold_in(keys[3], 71), 0)
    grad_codes = draw_grad_codes(jax.random.fold_in(keys[3], 71), 0)
    amax_history = draw_amax_history(jax.random.fold_in(keys[3], 71), 0)
    return {"act_codes": act_codes, "grad_codes": grad_codes, "amax_history": amax_history}


def decode(code_array):
    sign_bit = code_array // 128
    remainder = code_array % 128
    exponent_field = remainder // 8
    mantissa = 8 + remainder % 8
    multiplier = jnp.where(exponent_field >= 8, 8, jnp.where(exponent_field == 7, 4, jnp.where(exponent_field == 6, 2, 1)))
    signed = (1 - 2 * sign_bit) * mantissa * multiplier
    return (signed.astype(jnp.float32) * 0.03125).astype(jnp.bfloat16)


def quantize(values):
    magnitude = jnp.abs(values)
    step_size = jnp.full_like(values, 2.0 ** -9)
    for exponent in range(-5, 9):
        step_size = jnp.where(magnitude >= 2.0 ** exponent, step_size * 2.0, step_size)
    grid_value = jnp.minimum(jnp.floor(magnitude / step_size + 0.5) * step_size, 448.0)
    return jnp.sign(values) * grid_value


def scale_pair(peak):
    scale = peak * 0.0 + 2.0 ** 24
    inverse = peak * 0.0 + 2.0 ** -24
    for exponent in range(-16, 24):
        above = peak > 2.0 ** exponent
        scale = jnp.where(above, scale * 0.5, scale)
        inverse = jnp.where(above, inverse * 2.0, inverse)
    return scale, inverse


def reference(act_codes, grad_codes, amax_history):
    scale, inverse = scale_pair(jnp.max(amax_history))
    output_grad = decode(grad_codes).reshape(N_DP, TOK_DEV, PANEL).astype(jnp.float32)
    block_rows = FF // (4 * N_TENSOR)

    def one_block(index):
        code_block = lax.dynamic_slice_in_dim(act_codes, index * block_rows, block_rows, 1)
        activations = decode(code_block).reshape(N_DP, TOK_DEV, block_rows).astype(jnp.float32)
        partial_value = jnp.einsum("rtf,rtd->rfd", activations, output_grad, precision=lax.Precision.HIGHEST)
        block_peak = jnp.max(jnp.abs(partial_value), axis=(1, 2))
        level = quantize(partial_value * scale).astype(jnp.bfloat16)
        for section in range(LEVELS):
            half = level.shape[0] // 2
            total = level[:half].astype(jnp.float32) + level[half:].astype(jnp.float32)
            level = quantize(total * 0.5).astype(jnp.bfloat16)
        return level[0].astype(jnp.float32) * inverse, block_peak

    indices = jnp.arange(4 * N_TENSOR, dtype=jnp.int32)
    blocks, peaks = lax.map(one_block, indices)
    weight_grad = blocks.reshape(FF, PANEL)
    current_amax = jnp.max(peaks.reshape(N_TENSOR, 4, N_DP), axis=1).T.reshape(RANKS)
    new_history = jnp.concatenate([current_amax[:, None], amax_history[:, :-1]], axis=1)
    return weight_grad, new_history
```

```python
import functools

import jax
import jax.numpy as jnp
from jax import lax
from jax.experimental import pallas as pl
from jax.experimental.pallas import tpu as pltpu
from jax.sharding import PartitionSpec as P

MESH = pl.DeviceIdType.MESH
CHUNKS = 14
AHEAD = 3
NUDGE = 1.0 + 2.0 ** (-20)


def decode(codes):
    magnitude = (8 + (codes & 7)) << (((codes >> 3) & 15) - 5)
    return jnp.where(codes >= 128, -magnitude, magnitude).astype(jnp.float32) * 0.03125


def first_quant(partial, nudged_scale, big_scale):
    big = partial * big_scale
    rounded = (partial * nudged_scale + big) - big
    return jnp.minimum(jnp.maximum(rounded, -448.0), 448.0)


def mean_quant(a, b):
    total = a + b
    big = jnp.maximum(jnp.abs(total) * 2.0**19, 24576.0)
    return (total * (0.5 * NUDGE) + big) - big


def scale_pair(peak):
    scale = peak * 0.0 + 2.0**24
    inverse = peak * 0.0 + 2.0 ** (-24)
    for exponent in range(-16, 24):
        above = peak > 2.0**exponent
        scale = jnp.where(above, scale * 0.5, scale)
        inverse = jnp.where(above, inverse * 2.0, inverse)
    return (scale, inverse)


def kernel(n_dp, n_tensor, scales, act_hbm, grad_codes, keep_hbm, send_hbm, peaks,
           acts, grads, own_grads, code_slots, out_slots,
           code_sem, own_sem, out_sem,
           near_send, near_recv, far_send, far_recv,
           col_send, col_recv, row_send, row_recv):
    rest = n_dp // 4
    place = lax.axis_index("dp")
    t = lax.axis_index("tensor")
    hi = lax.div(place, rest)
    lo = lax.rem(place, rest)
    across = hi + 1 - 2 * lax.rem(hi, 2)
    along = hi + 2 - 4 * lax.div(hi, 2)
    upper = lax.div(lo * 2, rest)
    tokens = acts.shape[2]
    ff = acts.shape[1]
    size = ff // CHUNKS
    half_size = size // 2
    width = grads.shape[2]
    half_width = width // 2
    own_rows = tokens // n_tensor

    def group(member):
        return (member * rest + lo, t)

    def other(member, shift, n):
        return lax.rem(member + shift, n)

    barrier = pltpu.get_barrier_semaphore()
    for shift in range(1, 4):
        pl.semaphore_signal(barrier, inc=1, device_id=group(other(hi, shift, 4)), device_id_type=MESH)
    for shift in range(1, n_tensor):
        pl.semaphore_signal(barrier, inc=1, device_id=(place, other(t, shift, n_tensor)), device_id_type=MESH)

    def fetch(j):
        columns = pl.ds(pl.multiple_of(j * size, size), size)
        slot = lax.rem(j, 2)
        return pltpu.make_async_copy(act_hbm.at[:, columns], code_slots.at[slot], code_sem.at[slot])

    fetch(0).start()
    fetch(1).start()

    def near(j, owner, target, way):
        part = acts.at[owner, pl.ds(pl.multiple_of(j * size, size), size)]
        return pltpu.make_async_remote_copy(
            src_ref=part, dst_ref=part, send_sem=near_send.at[way, j], recv_sem=near_recv.at[way, j],
            device_id=group(target), device_id_type=MESH)

    def far(j, owner, target, way):
        start = pl.multiple_of(j * size + way * half_size, half_size)
        part = acts.at[owner, pl.ds(start, half_size)]
        return pltpu.make_async_remote_copy(
            src_ref=part, dst_ref=part, send_sem=far_send.at[way, j], recv_sem=far_recv.at[way, j],
            device_id=group(target), device_id_type=MESH)

    def prepare(j):
        fetch(j).wait()
        slot = lax.rem(j, 2)

        @pl.loop(0, size // 128)
        def _(i):
            block = code_slots[slot, :, pl.ds(pl.multiple_of(i * 128, 128), 128)]
            rows = pl.ds(pl.multiple_of(j * size + i * 128, 128), 128)
            acts[hi, rows, :] = decode(block).T.astype(jnp.bfloat16)

        @pl.when(j + 2 < CHUNKS)
        def _():
            fetch(j + 2).start()

        near(j, hi, across, 0).start()
        near(j, hi, along, 1).start()

    def forward(j):
        near(j, across, across, 0).wait_recv()
        far(j, across, along, 0).start()
        near(j, along, along, 1).wait_recv()
        far(j, along, across, 1).start()

    for member in range(4):
        @pl.loop(0, own_rows // 16)
        def _(i):
            rows = pl.ds(pl.multiple_of(i * 16, 16), 16)
            block = grad_codes[rows, member * width:(member + 1) * width]
            own_grads[member, rows, :] = decode(block).astype(jnp.bfloat16)

    pl.semaphore_wait(barrier, 3 + n_tensor - 1)

    own_slice = pl.ds(pl.multiple_of(t * own_rows, own_rows), own_rows)

    def columns_copy(source, target, owner, shift):
        return pltpu.make_async_remote_copy(
            src_ref=own_grads.at[source], dst_ref=grads.at[owner, own_slice],
            send_sem=col_send.at[shift - 1], recv_sem=col_recv.at[shift - 1],
            device_id=group(target), device_id_type=MESH)

    for shift in range(1, 4):
        target = other(hi, shift, 4)
        columns_copy(target, target, hi, shift).start()
    own = pltpu.make_async_copy(own_grads.at[hi], grads.at[hi, own_slice], own_sem)
    own.start()

    def early(j, carry):
        prepare(j)
        return carry

    lax.fori_loop(0, 1, early, 0)
    for shift in range(1, 4):
        source = other(hi, 4 - shift, 4)
        columns_copy(hi, source, source, shift).wait_recv()
    own.wait()

    def rows_copy(target, owner, shift):
        part = grads.at[:, pl.ds(pl.multiple_of(owner * own_rows, own_rows), own_rows)]
        return pltpu.make_async_remote_copy(
            src_ref=part, dst_ref=part, send_sem=row_send.at[shift - 1], recv_sem=row_recv.at[shift - 1],
            device_id=(place, target), device_id_type=MESH)

    for shift in range(1, n_tensor):
        rows_copy(other(t, shift, n_tensor), t, shift).start()
    lax.fori_loop(1, AHEAD, early, 0)
    forward(0)
    for shift in range(1, n_tensor):
        source = other(t, n_tensor - shift, n_tensor)
        rows_copy(source, source, shift).wait_recv()

    peaks[...] = jnp.zeros_like(peaks)
    nudged_scale = scales[0]
    big_scale = scales[1]
    tile_rows = min(256, size)
    tile_columns = min(256, half_width)
    row_tiles = size // tile_rows
    column_tiles = half_width // tile_columns

    def result(j, which):
        slot = lax.rem(j, 2)
        rows = pl.ds(pl.multiple_of(j * size, size), size)
        if which == 0:
            return pltpu.make_async_copy(out_slots.at[slot, upper], keep_hbm.at[rows], out_sem.at[slot, 0])
        return pltpu.make_async_copy(out_slots.at[slot, 1 - upper], send_hbm.at[rows], out_sem.at[slot, 1])

    def compute(j):
        slot = lax.rem(j, 2)

        @pl.loop(0, 2 * row_tiles * column_tiles)
        def _(index):
            half = lax.div(index, row_tiles * column_tiles)
            inner = lax.rem(index, row_tiles * column_tiles)
            row = pl.multiple_of(lax.div(inner, column_tiles) * tile_rows, tile_rows)
            column = pl.multiple_of(lax.rem(inner, column_tiles) * tile_columns, tile_columns)
            source_rows = pl.ds(pl.multiple_of(j * size + row, tile_rows), tile_rows)
            source_columns = pl.ds(pl.multiple_of(half * half_width + column, tile_columns), tile_columns)
            level = []
            for member in range(4):
                partial = jnp.dot(acts[member, source_rows, :], grads[member, :, source_columns],
                                  preferred_element_type=jnp.float32)
                size_8 = jnp.abs(partial).reshape(tile_rows // 8, 8, tile_columns)
                peaks[member] = jnp.maximum(peaks[member], jnp.max(size_8, axis=0))
                level.append(first_quant(partial, nudged_scale, big_scale))
            first = mean_quant(level[0], level[2])
            second = mean_quant(level[1], level[3])
            out_slots[slot, half, pl.ds(row, tile_rows), pl.ds(column, tile_columns)] = (
                mean_quant(first, second).astype(jnp.bfloat16))

    def step(j, carry):
        @pl.when(j + AHEAD < CHUNKS)
        def _():
            prepare(j + AHEAD)

        @pl.when(j + 1 < CHUNKS)
        def _():
            forward(j + 1)

        diagonal = 3 - hi
        far(j, diagonal, along, 0).wait_recv()
        far(j, diagonal, across, 1).wait_recv()

        @pl.when(j >= 2)
        def _():
            result(j - 2, 0).wait()
            result(j - 2, 1).wait()

        compute(j)
        result(j, 0).start()
        result(j, 1).start()
        return carry

    lax.fori_loop(0, CHUNKS, step, 0)

    def finish(j, carry):
        near(j, hi, across, 0).wait_send()
        near(j, hi, along, 1).wait_send()
        far(j, across, along, 0).wait_send()
        far(j, along, across, 1).wait_send()
        return carry

    lax.fori_loop(0, CHUNKS, finish, 0)
    for j in (CHUNKS - 2, CHUNKS - 1):
        result(j, 0).wait()
        result(j, 1).wait()
    for shift in range(1, 4):
        target = other(hi, shift, 4)
        columns_copy(target, target, hi, shift).wait_send()
    for shift in range(1, n_tensor):
        rows_copy(other(t, shift, n_tensor), t, shift).wait_send()


def two_levels(n_dp, n_tensor, scales, act_codes, grad_codes):
    tokens, ff = act_codes.shape
    own_rows, panel = grad_codes.shape
    width = panel // 4
    size = ff // CHUNKS
    tile_columns = min(256, width // 2)
    dma = pltpu.SemaphoreType.DMA
    return pl.pallas_call(
        functools.partial(kernel, n_dp, n_tensor),
        out_shape=[
            jax.ShapeDtypeStruct((ff, width // 2), jnp.bfloat16),
            jax.ShapeDtypeStruct((ff, width // 2), jnp.bfloat16),
            jax.ShapeDtypeStruct((4, 8, tile_columns), jnp.float32),
        ],
        in_specs=[
            pl.BlockSpec(memory_space=pltpu.SMEM),
            pl.BlockSpec(memory_space=pl.ANY),
            pl.BlockSpec(memory_space=pltpu.VMEM),
        ],
        out_specs=[
            pl.BlockSpec(memory_space=pl.ANY),
            pl.BlockSpec(memory_space=pl.ANY),
            pl.BlockSpec(memory_space=pltpu.VMEM),
        ],
        scratch_shapes=[
            pltpu.VMEM((4, ff, tokens), jnp.bfloat16),
            pltpu.VMEM((4, tokens, width), jnp.bfloat16),
            pltpu.VMEM((4, own_rows, width), jnp.bfloat16),
            pltpu.VMEM((2, tokens, size), jnp.int32),
            pltpu.VMEM((2, 2, size, width // 2), jnp.bfloat16),
            dma((2,)), dma(()), dma((2, 2)),
            dma((2, CHUNKS)), dma((2, CHUNKS)), dma((2, CHUNKS)), dma((2, CHUNKS)),
            dma((3,)), dma((3,)), dma((n_tensor - 1,)), dma((n_tensor - 1,)),
        ],
        compiler_params=pltpu.CompilerParams(
            collective_id=0, has_side_effects=True, vmem_limit_bytes=56 * 2**20
        ),
        cost_estimate=pl.CostEstimate(
            flops=8 * tokens * ff * width, bytes_accessed=4 * tokens * ff + 2 * ff * width, transcendentals=0
        ),
    )(scales, act_codes, grad_codes)


def shards(n_dp, n_tensor, act_codes, grad_codes, amax_history):
    history_top = lax.pmax(jnp.max(amax_history), ("dp", "tensor"))
    scale, inverse = scale_pair(history_top)
    scales = jnp.stack([scale * NUDGE, scale * 2.0**20])
    kept, outgoing, peaks = two_levels(n_dp, n_tensor, scales, act_codes, grad_codes)

    rest = n_dp // 4
    place = lax.axis_index("dp")
    group_peaks = jnp.max(peaks, axis=(1, 2))
    mine = jnp.arange(n_dp) % rest == place % rest
    all_peaks = lax.pmax(jnp.where(mine, jnp.repeat(group_peaks, rest), 0.0), "dp")
    own_peak = lax.dynamic_slice_in_dim(all_peaks, place, 1, 0)
    new_history = jnp.concatenate([own_peak.reshape(1, 1), amax_history[:, :-1]], axis=1)

    stride = rest // 2
    while True:
        arrived = lax.ppermute(outgoing, "dp", [(i, i ^ stride) for i in range(n_dp)])
        level = mean_quant(kept.astype(jnp.float32), arrived.astype(jnp.float32))
        stride //= 2
        if stride == 0:
            break
        level = level.astype(jnp.bfloat16)
        half = level.shape[1] // 2
        upper = place // stride % 2
        kept = lax.dynamic_slice_in_dim(level, upper * half, half, 1)
        outgoing = lax.dynamic_slice_in_dim(level, (1 - upper) * half, half, 1)
    return (level * inverse, new_history)


def solution(mesh):
    return jax.shard_map(
        functools.partial(shards, mesh.shape["dp"], mesh.shape["tensor"]),
        mesh=mesh,
        in_specs=(P("dp", "tensor"), P(("dp", "tensor"), None), P(("dp", "tensor"), None)),
        out_specs=(P("tensor", "dp"), P(("dp", "tensor"), None)),
        check_vma=False,
    )
```

```python
import functools

import jax
import jax.numpy as jnp
from jax import lax
from jax.experimental import pallas as pl
from jax.experimental.pallas import tpu as pltpu
from jax.sharding import PartitionSpec as P

MESH = pl.DeviceIdType.MESH
CHUNKS = 14
AHEAD = 5
RELAY = 2
LAG = 4
NUDGE = 1.0 + 2.0 ** (-20)


def decode(codes):
    magnitude = (8 + (codes & 7)) << (((codes >> 3) & 15) - 5)
    return jnp.where(codes >= 128, -magnitude, magnitude).astype(jnp.float32) * 0.03125


def first_quant(partial, nudged_scale, big_scale):
    big = partial * big_scale
    rounded = (partial * nudged_scale + big) - big
    return jnp.minimum(jnp.maximum(rounded, -448.0), 448.0)


def mean_quant(a, b):
    total = a + b
    big = jnp.maximum(jnp.abs(total) * 2.0**19, 24576.0)
    return (total * (0.5 * NUDGE) + big) - big


def scale_pair(peak):
    scale = peak * 0.0 + 2.0**24
    inverse = peak * 0.0 + 2.0 ** (-24)
    for exponent in range(-16, 24):
        above = peak > 2.0**exponent
        scale = jnp.where(above, scale * 0.5, scale)
        inverse = jnp.where(above, inverse * 2.0, inverse)
    return (scale, inverse)


def kernel(n_dp, n_tensor, act_hbm, grad_codes, history, keep_hbm, arrive_hbm, amax_out, inverse_out,
           acts, grads, own_grads, code_slots, out_slots,
           peaks, peaks_in, tops_hi, tops_t, tops_lo,
           code_sem, own_sem, out_sem,
           near_send, near_recv, far_send, far_recv,
           col_send, col_recv, row_send, row_recv, pair_send, pair_recv,
           hi_send, hi_recv, t_send, t_recv, lo_send, lo_recv, peak_send, peak_recv):
    rest = n_dp // 4
    place = lax.axis_index("dp")
    t = lax.axis_index("tensor")
    hi = lax.div(place, rest)
    lo = lax.rem(place, rest)
    across = hi + 1 - 2 * lax.rem(hi, 2)
    along = hi + 2 - 4 * lax.div(hi, 2)
    upper = lax.div(lo * 2, rest)
    tokens = acts.shape[2]
    ff = acts.shape[1]
    size = ff // CHUNKS
    half_size = size // 2
    width = grads.shape[2]
    half_width = width // 2
    own_rows = tokens // n_tensor

    def group(member):
        return (member * rest + lo, t)

    def other(member, shift, n):
        return lax.rem(member + shift, n)

    barrier = pltpu.get_barrier_semaphore()
    for shift in range(1, 4):
        pl.semaphore_signal(barrier, inc=1, device_id=group(other(hi, shift, 4)), device_id_type=MESH)
    for shift in range(1, n_tensor):
        pl.semaphore_signal(barrier, inc=1, device_id=(place, other(t, shift, n_tensor)), device_id_type=MESH)
    for shift in range(1, rest):
        pl.semaphore_signal(barrier, inc=1, device_id=(hi * rest + other(lo, shift, rest), t), device_id_type=MESH)

    def fetch(j):
        columns = pl.ds(pl.multiple_of(j * size, size), size)
        slot = lax.rem(j, 2)
        return pltpu.make_async_copy(act_hbm.at[:, columns], code_slots.at[slot], code_sem.at[slot])

    fetch(0).start()
    fetch(1).start()

    def near(j, owner, target, way):
        part = acts.at[owner, pl.ds(pl.multiple_of(j * size, size), size)]
        return pltpu.make_async_remote_copy(
            src_ref=part, dst_ref=part, send_sem=near_send.at[way, j], recv_sem=near_recv.at[way, j],
            device_id=group(target), device_id_type=MESH)

    def far(j, owner, target, way):
        start = pl.multiple_of(j * size + way * half_size, half_size)
        part = acts.at[owner, pl.ds(start, half_size)]
        return pltpu.make_async_remote_copy(
            src_ref=part, dst_ref=part, send_sem=far_send.at[way, j], recv_sem=far_recv.at[way, j],
            device_id=group(target), device_id_type=MESH)

    def prepare(j):
        fetch(j).wait()
        slot = lax.rem(j, 2)

        @pl.loop(0, size // 128)
        def _(i):
            block = code_slots[slot, :, pl.ds(pl.multiple_of(i * 128, 128), 128)]
            rows = pl.ds(pl.multiple_of(j * size + i * 128, 128), 128)
            acts[hi, rows, :] = decode(block).T.astype(jnp.bfloat16)

        @pl.when(j + 2 < CHUNKS)
        def _():
            fetch(j + 2).start()

        near(j, hi, across, 0).start()
        near(j, hi, along, 1).start()

    def forward(j):
        near(j, across, across, 0).wait_recv()
        far(j, across, along, 0).start()
        near(j, along, along, 1).wait_recv()
        far(j, along, across, 1).start()

    for member in range(4):
        @pl.loop(0, own_rows // 16)
        def _(i):
            rows = pl.ds(pl.multiple_of(i * 16, 16), 16)
            block = grad_codes[rows, member * width:(member + 1) * width]
            own_grads[member, rows, :] = decode(block).astype(jnp.bfloat16)

    pl.semaphore_wait(barrier, 3 + n_tensor - 1 + rest - 1)

    def top_copy(tops, source, target, shift, send, recv):
        return pltpu.make_async_remote_copy(
            src_ref=tops.at[source], dst_ref=tops.at[source],
            send_sem=send.at[shift - 1], recv_sem=recv.at[shift - 1],
            device_id=target, device_id_type=MESH)

    stages = (
        (tops_hi, hi, 4, group, hi_send, hi_recv),
        (tops_t, t, n_tensor, lambda member: (place, member), t_send, t_recv),
        (tops_lo, lo, rest, lambda member: (hi * rest + member, t), lo_send, lo_recv),
    )

    def top_start(stage, value):
        tops, index, n, device, send, recv = stages[stage]
        tops[index] = value
        for shift in range(1, n):
            top_copy(tops, index, device(other(index, shift, n)), shift, send, recv).start()

    def top_finish(stage):
        tops, index, n, device, send, recv = stages[stage]
        for shift in range(1, n):
            source = other(index, n - shift, n)
            top_copy(tops, source, device(source), shift, send, recv).wait_recv()
        return jnp.max(tops[...], axis=0)

    top_start(0, jnp.broadcast_to(jnp.max(history[...]), (8, 128)))

    own_slice = pl.ds(pl.multiple_of(t * own_rows, own_rows), own_rows)

    def columns_copy(source, target, owner, shift):
        return pltpu.make_async_remote_copy(
            src_ref=own_grads.at[source], dst_ref=grads.at[owner, own_slice],
            send_sem=col_send.at[shift - 1], recv_sem=col_recv.at[shift - 1],
            device_id=group(target), device_id_type=MESH)

    for shift in range(1, 4):
        target = other(hi, shift, 4)
        columns_copy(target, target, hi, shift).start()
    own = pltpu.make_async_copy(own_grads.at[hi], grads.at[hi, own_slice], own_sem)
    own.start()

    def early(j, carry):
        prepare(j)
        return carry

    lax.fori_loop(0, 1, early, 0)
    for shift in range(1, 4):
        source = other(hi, 4 - shift, 4)
        columns_copy(hi, source, source, shift).wait_recv()
    own.wait()

    def rows_copy(piece, target, way):
        part = grads.at[:, pl.ds(pl.multiple_of(piece * own_rows, own_rows), own_rows)]
        return pltpu.make_async_remote_copy(
            src_ref=part, dst_ref=part, send_sem=row_send.at[way, piece], recv_sem=row_recv.at[piece],
            device_id=(place, target), device_id_type=MESH)

    has_up = t + 1 < n_tensor
    has_down = t >= 1
    up = lax.rem(t + 1, n_tensor)
    down = lax.rem(t + n_tensor - 1, n_tensor)

    def rows_step(hop):
        @pl.when(t >= hop)
        def _():
            piece = t - hop
            if hop:
                rows_copy(piece, down, 0).wait_recv()

            @pl.when(has_up)
            def _():
                rows_copy(piece, up, 0).start()

        @pl.when(t + hop < n_tensor)
        def _():
            piece = t + hop
            if hop:
                rows_copy(piece, up, 1).wait_recv()

            @pl.when(has_down)
            def _():
                rows_copy(piece, down, 1).start()

    rows_step(0)
    lax.fori_loop(1, AHEAD, early, 0)
    top_start(1, top_finish(0))
    for j in range(RELAY):
        forward(j)
    top_start(2, top_finish(1))

    def move(j):
        @pl.when(j + AHEAD < CHUNKS)
        def _():
            prepare(j + AHEAD)

        @pl.when(j + RELAY < CHUNKS)
        def _():
            forward(j + RELAY)

    for j in range(LAG):
        move(j)
        if j + 1 < n_tensor:
            rows_step(j + 1)
    for hop in range(LAG + 1, n_tensor):
        rows_step(hop)

    scale, inverse = scale_pair(top_finish(2))
    inverse_out[...] = inverse
    nudged_scale = jnp.max(scale) * NUDGE
    big_scale = jnp.max(scale) * 2.0**20
    peaks[...] = jnp.zeros_like(peaks)
    tile_rows = min(256, size)
    tile_columns = min(256, half_width)
    row_tiles = size // tile_rows
    column_tiles = half_width // tile_columns

    def result(j, which):
        slot = lax.rem(j, 2)
        rows = pl.ds(pl.multiple_of(j * size, size), size)
        if which == 0:
            return pltpu.make_async_copy(out_slots.at[slot, upper], keep_hbm.at[rows], out_sem.at[slot])
        return pltpu.make_async_remote_copy(
            src_ref=out_slots.at[slot, 1 - upper], dst_ref=arrive_hbm.at[rows],
            send_sem=pair_send.at[slot], recv_sem=pair_recv.at[j],
            device_id=(hi * rest + lo + (rest // 2) * (1 - 2 * upper), t), device_id_type=MESH)

    def compute(j):
        slot = lax.rem(j, 2)

        @pl.loop(0, 2 * row_tiles * column_tiles)
        def _(index):
            half = lax.div(index, row_tiles * column_tiles)
            inner = lax.rem(index, row_tiles * column_tiles)
            row = pl.multiple_of(lax.div(inner, column_tiles) * tile_rows, tile_rows)
            column = pl.multiple_of(lax.rem(inner, column_tiles) * tile_columns, tile_columns)
            source_rows = pl.ds(pl.multiple_of(j * size + row, tile_rows), tile_rows)
            source_columns = pl.ds(pl.multiple_of(half * half_width + column, tile_columns), tile_columns)
            level = []
            for member in range(4):
                partial = jnp.dot(acts[member, source_rows, :], grads[member, :, source_columns],
                                  preferred_element_type=jnp.float32)
                size_8 = jnp.abs(partial).reshape(tile_rows // 8, 8, tile_columns)
                peaks[member] = jnp.maximum(peaks[member], jnp.max(size_8, axis=0))
                level.append(first_quant(partial, nudged_scale, big_scale))
            first = mean_quant(level[0], level[2])
            second = mean_quant(level[1], level[3])
            out_slots[slot, half, pl.ds(row, tile_rows), pl.ds(column, tile_columns)] = (
                mean_quant(first, second).astype(jnp.bfloat16))

    def chunk(j):
        diagonal = 3 - hi
        far(j, diagonal, along, 0).wait_recv()
        far(j, diagonal, across, 1).wait_recv()

        @pl.when(j >= 2)
        def _():
            result(j - 2, 0).wait()
            result(j - 2, 1).wait_send()

        compute(j)
        result(j, 0).start()
        result(j, 1).start()

    def catch_up(j, carry):
        move(j)

        @pl.loop(0, 2)
        def _(i):
            chunk(2 * (j - LAG) + i)
        return carry

    def step(j, carry):
        move(j)
        chunk(j)
        return carry

    lax.fori_loop(LAG, 2 * LAG, catch_up, 0)
    lax.fori_loop(2 * LAG, CHUNKS, step, 0)

    def peak_copy(target, owner, shift):
        return pltpu.make_async_remote_copy(
            src_ref=peaks.at[target], dst_ref=peaks_in.at[owner],
            send_sem=peak_send.at[shift - 1], recv_sem=peak_recv.at[shift - 1],
            device_id=group(target), device_id_type=MESH)

    for shift in range(1, 4):
        peak_copy(other(hi, shift, 4), hi, shift).start()
    peaks_in[hi] = peaks[hi]

    def finish(j, carry):
        near(j, hi, across, 0).wait_send()
        near(j, hi, along, 1).wait_send()
        far(j, across, along, 0).wait_send()
        far(j, along, across, 1).wait_send()
        result(j, 1).wait_recv()
        return carry

    lax.fori_loop(0, CHUNKS, finish, 0)
    for j in (CHUNKS - 2, CHUNKS - 1):
        result(j, 0).wait()
        result(j, 1).wait_send()
    for shift in range(1, 4):
        target = other(hi, shift, 4)
        columns_copy(target, target, hi, shift).wait_send()
        peak_copy(target, hi, shift).wait_send()
        source = other(hi, 4 - shift, 4)
        peak_copy(source, source, shift).wait_recv()
    amax_out[...] = jnp.broadcast_to(jnp.max(peaks_in[...]), (8, 128))
    for hop in range(n_tensor):
        @pl.when((t >= hop) & has_up)
        def _():
            rows_copy(t - hop, up, 0).wait_send()

        @pl.when((t + hop < n_tensor) & has_down)
        def _():
            rows_copy(t + hop, down, 1).wait_send()
    for tops, index, n, device, send, recv in stages:
        for shift in range(1, n):
            top_copy(tops, index, device(other(index, shift, n)), shift, send, recv).wait_send()


def two_levels(n_dp, n_tensor, act_codes, grad_codes, amax_history):
    tokens, ff = act_codes.shape
    own_rows, panel = grad_codes.shape
    width = panel // 4
    rest = n_dp // 4
    size = ff // CHUNKS
    tile_columns = min(256, width // 2)
    dma = pltpu.SemaphoreType.DMA
    return pl.pallas_call(
        functools.partial(kernel, n_dp, n_tensor),
        out_shape=[
            jax.ShapeDtypeStruct((ff, width // 2), jnp.bfloat16),
            jax.ShapeDtypeStruct((ff, width // 2), jnp.bfloat16),
            jax.ShapeDtypeStruct((8, 128), jnp.float32),
            jax.ShapeDtypeStruct((8, 128), jnp.float32),
        ],
        in_specs=[
            pl.BlockSpec(memory_space=pl.ANY),
            pl.BlockSpec(memory_space=pltpu.VMEM),
            pl.BlockSpec(memory_space=pltpu.VMEM),
        ],
        out_specs=[
            pl.BlockSpec(memory_space=pl.ANY),
            pl.BlockSpec(memory_space=pl.ANY),
            pl.BlockSpec(memory_space=pltpu.VMEM),
            pl.BlockSpec(memory_space=pltpu.VMEM),
        ],
        scratch_shapes=[
            pltpu.VMEM((4, ff, tokens), jnp.bfloat16),
            pltpu.VMEM((4, tokens, width), jnp.bfloat16),
            pltpu.VMEM((4, own_rows, width), jnp.bfloat16),
            pltpu.VMEM((2, tokens, size), jnp.int32),
            pltpu.VMEM((2, 2, size, width // 2), jnp.bfloat16),
            pltpu.VMEM((4, 8, tile_columns), jnp.float32),
            pltpu.VMEM((4, 8, tile_columns), jnp.float32),
            pltpu.VMEM((4, 8, 128), jnp.float32),
            pltpu.VMEM((n_tensor, 8, 128), jnp.float32),
            pltpu.VMEM((rest, 8, 128), jnp.float32),
            dma((2,)), dma(()), dma((2,)),
            dma((2, CHUNKS)), dma((2, CHUNKS)), dma((2, CHUNKS)), dma((2, CHUNKS)),
            dma((3,)), dma((3,)), dma((2, n_tensor)), dma((n_tensor,)), dma((2,)), dma((CHUNKS,)),
            dma((3,)), dma((3,)), dma((n_tensor - 1,)), dma((n_tensor - 1,)),
            dma((rest - 1,)), dma((rest - 1,)), dma((3,)), dma((3,)),
        ],
        compiler_params=pltpu.CompilerParams(
            collective_id=0, has_side_effects=True, vmem_limit_bytes=56 * 2**20
        ),
        cost_estimate=pl.CostEstimate(
            flops=8 * tokens * ff * width, bytes_accessed=4 * tokens * ff + 2 * ff * width, transcendentals=0
        ),
    )(act_codes, grad_codes, amax_history)


def shards(n_dp, n_tensor, act_codes, grad_codes, amax_history):
    kept, arrived, amax, inverse = two_levels(n_dp, n_tensor, act_codes, grad_codes, amax_history)
    new_history = jnp.concatenate([amax[:1, :1], amax_history[:, :-1]], axis=1)
    rest = n_dp // 4
    place = lax.axis_index("dp")
    stride = rest // 2
    while True:
        level = mean_quant(kept.astype(jnp.float32), arrived.astype(jnp.float32))
        stride //= 2
        if stride == 0:
            break
        level = level.astype(jnp.bfloat16)
        half = level.shape[1] // 2
        upper = place // stride % 2
        kept = lax.dynamic_slice_in_dim(level, upper * half, half, 1)
        outgoing = lax.dynamic_slice_in_dim(level, (1 - upper) * half, half, 1)
        arrived = lax.ppermute(outgoing, "dp", [(i, i ^ stride) for i in range(n_dp)])
    return (level * inverse[0, 0], new_history)


def solution(mesh):
    return jax.shard_map(
        functools.partial(shards, mesh.shape["dp"], mesh.shape["tensor"]),
        mesh=mesh,
        in_specs=(P("dp", "tensor"), P(("dp", "tensor"), None), P(("dp", "tensor"), None)),
        out_specs=(P("tensor", "dp"), P(("dp", "tensor"), None)),
        check_vma=False,
    )
```
